512 devices in a mesh: node: 32 (over y, x, core), head: 16 (over z).
Axes of the slice: x: 4, y: 4, z: 16, core: 2. Of those that a mesh axis runs over, the one named last changes fastest.
Arguments:
- feats: bfloat16 [65536, 512], P('node'), may hold values from -13 to 13
- cot: bfloat16 [65536, 512], P(('node', 'head')), may hold values from -6 to 6
- wq: bfloat16 [512, 512], P(None, 'head'), may hold values from -0.25 to 0.25
- wk: bfloat16 [512, 512], P(None, 'head'), may hold values from -0.25 to 0.25
- wv: bfloat16 [512, 512], P(None, 'head'), may hold values from -0.25 to 0.25
- adj: int32 [512, 4], P('node'), may hold values from 0 to 15
- adj_count: int32 [512], P('node'), may hold values from 1 to 4
- perms: int32 [3, 32, 16], P(None, 'node'), may hold values from 0 to 15, each once within a row
Outputs:
- attn: bfloat16 [65536, 512], P(('node', 'head'))
- grad_x: bfloat16 [65536, 512], P(('node', 'head'))
- grad_wq: float32 [512, 512], P(None, 'head')
- grad_wk: float32 [512, 512], P(None, 'head')
- grad_wv: float32 [512, 512], P(None, 'head')
The draws below stay inside these ranges and needn't reach their ends.
Inputs may be any that keep to these rules, and one draw needn't show every extreme that they name: Only the first adj_count[b] entries of row b of adj are used; entries index blocks within the group of block b. Each row perms[m, n] holds every number below 16 once.
All inputs are finite; a program needn't handle non-finite values.
Results may differ from the reference program's by a relative error of at most 0.025.
The reference program's roundings to bfloat16 on the way count: a program that leaves them out, or rounds other values in their place, can miss the bound.
Values may be sent and summed in bfloat16 or wider, within the bound.
A program may use at most 64 MiB of HBM per device.

```python
import math
import jax
import jax.numpy as jnp
from jax import lax

D = 512
HEADS = 8
BLOCK = 128
MAXADJ = 4
MATCH = 3
GROUP = 16
NBLK = 512
NODES = 65536
N_NODE = 32


def draw_feats(key, part):
    key = jax.random.fold_in(key, 11)
    first = jax.random.fold_in(key, 0)
    return jnp.clip(jax.random.normal(first, (NODES, D), jnp.float32), -6.0, 6.0).astype(jnp.bfloat16)


def plant(drawn, stream_key, low, top_value):
    longest = drawn.shape.index(max(drawn.shape))
    spots = []
    for shift in (0, 1):
        where = [jax.random.randint(jax.random.fold_in(stream_key, axis), (), 0, length) for axis, length in enumerate(drawn.shape)]
        where[longest] = (where[longest] + shift) % drawn.shape[longest]
        spots.append(tuple(where))
    return drawn.at[spots[0]].set(low).at[spots[1]].set(top_value)


def shard_levels(own_key, extent, pieces, least, top_value):
    def one(position, blocks):
        heights = jax.random.uniform(jax.random.fold_in(jax.random.fold_in(own_key, 6), position), (blocks,), jnp.float32, least / len(pieces), top_value / len(pieces))
        return jnp.repeat(jnp.exp(heights), extent[position] // blocks).reshape((-1,) + (1,) * (len(extent) - position - 1))

    gain = one(*pieces[0])
    for cut in pieces[1:]:
        gain = gain * one(*cut)
    return gain


def noise(rng, shape, spread, most, shards=(), kind=jnp.bfloat16):
    entries = spread * jax.random.normal(rng, shape, jnp.float32)
    if shards:
        entries = entries * shard_levels(rng, shape, shards, -0.22, 0.18)
    return jnp.clip(entries, -most, most).astype(kind)


def setup_inputs(seed: int = 0) -> dict:
    key_list = jax.random.split(jax.random.key(seed), 9)
    feats = draw_feats(jax.random.fold_in(key_list[8], 71), 0)
    cot = noise(key_list[1], (NODES, D), 1.0, 6.0, ((0, 512),))
    wq = noise(key_list[2], (D, D), D ** -0.5, 0.25, ((1, 16),))
    wk = noise(key_list[3], (D, D), D ** -0.5, 0.25, ((1, 16),))
    wv = noise(key_list[4], (D, D), D ** -0.5, 0.25, ((1, 16),))
    adj = plant(jax.random.randint(key_list[5], (NBLK, MAXADJ), 0, GROUP), jax.random.fold_in(key_list[5], 1), 0, GROUP - 1).astype(jnp.int32)
    adj_count = plant(jax.random.randint(key_list[6], (NBLK,), 1, MAXADJ + 1), jax.random.fold_in(key_list[6], 1), 1, MAXADJ).astype(jnp.int32)
    perms = jax.vmap(lambda own: jax.random.permutation(own, GROUP))(jax.random.split(key_list[7], MATCH * N_NODE)).reshape((MATCH, N_NODE, GROUP)).astype(jnp.int32)
    return dict(feats=feats, cot=cot, wq=wq, wk=wk, wv=wv, adj=adj, adj_count=adj_count, perms=perms)


def block_pass(queries, keys, values, allowed, upstream):
    width = queries.shape[1]
    head_dim = width // HEADS
    scale = 1.0 / math.sqrt(head_dim)
    q_heads = queries.reshape(BLOCK, HEADS, head_dim).astype(jnp.float32)
    k_heads = keys.reshape(-1, HEADS, head_dim).astype(jnp.float32)
    v_heads = values.reshape(-1, HEADS, head_dim).astype(jnp.float32)
    g_heads = upstream.reshape(BLOCK, HEADS, head_dim).astype(jnp.float32)
    scores = jnp.einsum('qhd,khd->hqk', q_heads, k_heads) * scale
    scores = jnp.where(allowed[None, None, :], scores, -1e+30)
    top = lax.optimization_barrier(jnp.max(scores, axis=-1, keepdims=True))
    expo = jnp.exp(scores - top)
    prob = expo / lax.optimization_barrier(jnp.sum(expo, axis=-1, keepdims=True))
    prob_low = prob.astype(jnp.bfloat16).astype(jnp.float32)
    output = jnp.einsum('hqk,khd->qhd', prob_low, v_heads)
    d_values = jnp.einsum('hqk,qhd->khd', prob_low, g_heads)
    d_prob = jnp.einsum('qhd,khd->hqk', g_heads, v_heads)
    centre = lax.optimization_barrier(jnp.sum(prob * d_prob, axis=-1, keepdims=True))
    d_score = (prob * (d_prob - centre)).astype(jnp.bfloat16).astype(jnp.float32)
    d_query = jnp.einsum('hqk,khd->qhd', d_score, k_heads) * scale
    d_keys = jnp.einsum('hqk,qhd->khd', d_score, q_heads) * scale
    return (output.reshape(BLOCK, width).astype(jnp.bfloat16), d_query.reshape(BLOCK, width), d_keys.reshape(-1, width), d_values.reshape(-1, width))

def reference(feats, cot, wq, wk, wv, adj, adj_count, perms):
    width = feats.shape[1]
    total_blocks = feats.shape[0] // BLOCK
    slots = 1 + MAXADJ + MATCH
    q_all = jnp.dot(feats, wq, preferred_element_type=jnp.float32).astype(jnp.bfloat16)
    k_all = jnp.dot(feats, wk, preferred_element_type=jnp.float32).astype(jnp.bfloat16)
    v_all = jnp.dot(feats, wv, preferred_element_type=jnp.float32).astype(jnp.bfloat16)
    block_ids = jnp.arange(total_blocks, dtype=jnp.int32)
    base = block_ids // GROUP * GROUP
    partner = jnp.transpose(perms.reshape(MATCH, total_blocks)).astype(jnp.int32)
    slot_ids = jnp.concatenate([block_ids[:, None], base[:, None] + adj.astype(jnp.int32), base[:, None] + partner], axis=1)
    slot_pos = jnp.arange(slots, dtype=jnp.int32)
    listed = (slot_pos >= 1) & (slot_pos <= MAXADJ)
    allowed = jnp.logical_not(listed)[None, :] | (slot_pos[None, :] - 1 < adj_count.astype(jnp.int32)[:, None])
    allowed = jnp.repeat(allowed, BLOCK, axis=1)
    q_blocks = q_all.reshape(total_blocks, BLOCK, width)
    k_blocks = k_all.reshape(total_blocks, BLOCK, width)
    v_blocks = v_all.reshape(total_blocks, BLOCK, width)
    g_blocks = cot.reshape(total_blocks, BLOCK, width)

    def step(carry, item):
        acc_k, acc_v = carry
        query, upstream, indices, mask = item
        keys = k_blocks[indices].reshape(slots * BLOCK, width)
        values = v_blocks[indices].reshape(slots * BLOCK, width)
        output, d_query, d_keys, d_values = block_pass(query, keys, values, mask, upstream)
        acc_k = acc_k.at[indices].add(d_keys.reshape(slots, BLOCK, width))
        acc_v = acc_v.at[indices].add(d_values.reshape(slots, BLOCK, width))
        return ((acc_k, acc_v), (output, d_query))
    start = jnp.zeros((total_blocks, BLOCK, width), jnp.float32)
    (acc_k, acc_v), (outputs, d_queries) = lax.scan(step, (start, start), (q_blocks, g_blocks, slot_ids, allowed))
    grad_q = d_queries.reshape(-1, width).astype(jnp.bfloat16)
    grad_k = acc_k.reshape(-1, width).astype(jnp.bfloat16)
    grad_v = acc_v.reshape(-1, width).astype(jnp.bfloat16)
    grad_wq = jnp.dot(feats.T, grad_q, preferred_element_type=jnp.float32)
    grad_wk = jnp.dot(feats.T, grad_k, preferred_element_type=jnp.float32)
    grad_wv = jnp.dot(feats.T, grad_v, preferred_element_type=jnp.float32)
    grad_x = (jnp.dot(grad_q, wq.T, preferred_element_type=jnp.float32) + jnp.dot(grad_k, wk.T, preferred_element_type=jnp.float32) + jnp.dot(grad_v, wv.T, preferred_element_type=jnp.float32)).astype(jnp.bfloat16)
    attn = outputs.reshape(-1, width)
    return (attn, grad_x, grad_wq, grad_wk, grad_wv)
```

```python
import functools

import jax
import jax.numpy as jnp
from jax import lax
from jax.experimental import pallas as pl
from jax.experimental.pallas import tpu as pltpu
from jax.sharding import PartitionSpec as P

HEADS = 8
BLOCK = 128
MAXADJ = 4
MATCH = 3
SLOTS = 1 + MAXADJ + MATCH
HD = 64
CORES = 2
MESH = pl.DeviceIdType.MESH
VMEM_BYTES = 40 * 1024 * 1024
NT = (((1,), (1,)), ((), ()))


def vmem():
    return pl.BlockSpec(memory_space=pltpu.VMEM)


def hbm():
    return pl.BlockSpec(memory_space=pltpu.HBM)


def smem():
    return pl.BlockSpec(memory_space=pltpu.SMEM)


def low_lanes(rows):
    return lax.broadcasted_iota(jnp.int32, (rows, 128), 1) < HD


def plan_kernel(group, adj_ref, perms_ref, plan_ref, fill):
    order = group * SLOTS
    last = 2 * group * SLOTS
    for c in range(group):
        fill[c] = 0
    for b in range(group):
        for s in range(SLOTS):
            if s == 0:
                c = b
            elif s <= MAXADJ:
                c = adj_ref[s - 1, b]
            else:
                c = perms_ref[s - 1 - MAXADJ, 0, b]
            plan_ref[b * SLOTS + s] = c
            fill[c] = fill[c] + 1
    at = 0
    for c in range(group):
        n = fill[c]
        fill[c] = at
        at = at + n
        plan_ref[last + c] = at - 1
    for b in range(group):
        for s in range(SLOTS):
            c = plan_ref[b * SLOTS + s]
            at = fill[c]
            plan_ref[order + at] = b * SLOTS + s
            fill[c] = at + 1


def loop(first, stop, act):
    def body(d, carry):
        act(d)
        return carry

    lax.fori_loop(first, stop, body, 0)


def layer_kernel(ways, xs, ys, plan_hbm, counts_hbm, wq_hbm, wv_hbm, wk_hbm, cot_hbm, feats_hbm,
                 r1_ref, r2_ref, all_ref, out_ref,
                 plan, counts, cot, feats, shard, wb, packed, landed, kv, kvt, qs, terms, runs, t1, t2, left, gw,
                 near, line, in_sem, w_send, w_recv, c_send, c_recv, a_send, a_recv, p_send, p_recv, h_send, h_recv,
                 z_send, z_recv, n_send, n_recv, y_send, y_recv, g_send, g_recv):
    node = lax.axis_index("node")
    me = lax.axis_index("head")
    half = lax.rem(me, 2)
    head = me // 2
    partner = me + 1 - 2 * half
    cross = xs * CORES
    nodes = ys * cross
    y = node // cross
    near_me = lax.rem(node, cross)
    core = lax.rem(node, CORES)
    cols, width = wq_hbm.shape
    order = ways * SLOTS
    last = 2 * order
    reach = ways // 2
    barrier = pltpu.get_barrier_semaphore()

    def around(d):
        return (node, lax.rem(me + d, ways))

    def across(d):
        return (lax.rem(node + d, nodes), me)

    def remote(src, dst, send_sem, recv_sem, device):
        return pltpu.make_async_remote_copy(
            src_ref=src, dst_ref=dst, send_sem=send_sem, recv_sem=recv_sem, device_id=device, device_id_type=MESH)

    loop(1, ways, lambda d: pl.semaphore_signal(barrier, inc=1, device_id=around(d), device_id_type=MESH))
    loop(1, nodes, lambda d: pl.semaphore_signal(barrier, inc=1, device_id=across(d), device_id_type=MESH))
    inputs = [
        pltpu.make_async_copy(src, dst, in_sem.at[i])
        for i, (src, dst) in enumerate((
            (wq_hbm, shard.at[0]), (wv_hbm, shard.at[1]), (wk_hbm, shard.at[2]), (cot_hbm, cot),
            (plan_hbm, plan), (counts_hbm, counts), (feats_hbm, feats)))
    ]
    for copy in inputs:
        copy.start()
    for copy in inputs[:4]:
        copy.wait()
    wb[0] = jnp.zeros(wb.shape[1:], wb.dtype)
    wb[pl.ds(1, 3), half] = shard[...]
    low = low_lanes(64)
    for p in range(HEADS // 2):
        pair = cot[:, 128 * p:128 * (p + 1)].astype(jnp.float32)
        first, second = pair[:64], pair[64:]
        packed[2 * p] = jnp.where(low, first, pltpu.roll(second, 64, 1)).astype(jnp.bfloat16)
        packed[2 * p + 1] = jnp.where(low, pltpu.roll(first, 64, 1), second).astype(jnp.bfloat16)
    landed[me] = packed[head]
    pl.semaphore_wait(barrier, (ways - 1) + (nodes - 1))

    w_copy = remote(shard, wb.at[pl.ds(1, 3), half], w_send, w_recv, (node, partner))
    w_copy.start()

    def cot_copy(d):
        dest = lax.rem(me + d, ways)
        return remote(packed.at[dest // 2], landed.at[me], c_send.at[d], c_recv.at[d], (node, dest))

    def tile(n):
        x = lax.rem(n // CORES, xs)
        core = lax.rem(n, CORES)
        rows = cols // CORES
        return (n // cross, pl.ds(pl.multiple_of(core * rows, rows), rows), pl.ds(pl.multiple_of(x * 128, 128), 128))

    def shard_copy(d):
        t, rows, lanes = tile(node)
        return remote(shard.at[t, rows, lanes], all_ref.at[me, t, rows, lanes], a_send.at[d], a_recv.at[d], around(d))

    def plane_copy(n, d):
        t, rows, lanes = tile(n)
        piece = all_ref.at[:, t, rows, lanes]
        return remote(piece, piece, p_send.at[d], p_recv.at[d], across(CORES * d))

    def core_copy(c):
        rows = pl.ds(pl.multiple_of(c * (cols // CORES), cols // CORES), cols // CORES)
        piece = all_ref.at[:, :, rows, :]
        return remote(piece, piece, h_send, h_recv, (node + 1 - 2 * core, me))

    def start_cot(k):
        @pl.when(k > 0)
        def _():
            cot_copy(k).start()

        cot_copy(ways - 1 - k).start()

    loop(0, reach, start_cot)
    carries = y < 3

    @pl.when(carries)
    def _():
        t, rows, lanes = tile(node)
        all_ref[me, t, rows, lanes] = shard[t, rows, lanes]
        loop(1, ways, lambda d: shard_copy(d).start())

    for copy in inputs[4:]:
        copy.wait()
    w_copy.wait()
    weights = wb[...].reshape(4 * HD, width)
    per = 4
    for c in range(ways // per):
        rows = feats[c * per * BLOCK:(c + 1) * per * BLOCK, :]
        out = lax.dot_general(rows, weights, NT, preferred_element_type=jnp.float32)
        for j in range(per):
            b = c * per + j
            part = out[j * BLOCK:(j + 1) * BLOCK]
            qs[b] = (part[:, :128].astype(jnp.bfloat16).astype(jnp.float32) * 0.125).astype(jnp.bfloat16)
            kv[b] = part[:, 128:].astype(jnp.bfloat16)
            kvt[b] = jnp.transpose(part[:, 128:]).astype(jnp.bfloat16)

    def block(b):
        ids = [plan[b * SLOTS + s] for s in range(SLOTS)]
        count = counts[b]
        keys = jnp.concatenate([kv[i] for i in ids], axis=0)
        keys_t = jnp.concatenate([kvt[i] for i in ids], axis=1)
        got = landed[b].astype(jnp.float32)
        cot_rows = jnp.concatenate(
            [jnp.where(low, got, 0.0), jnp.where(low, pltpu.roll(got, 64, 1), 0.0)], axis=0).astype(jnp.bfloat16)
        qc = jnp.concatenate([qs[b], cot_rows], axis=0)
        both = lax.dot_general(keys, qc, NT, preferred_element_type=jnp.float32)
        scores = both[:, :BLOCK]
        d_prob = both[:, BLOCK:]
        bias = jnp.concatenate(
            [jnp.full((BLOCK, 1), jnp.where(s <= count, 0.0, -1e30) if 1 <= s <= MAXADJ else 0.0, jnp.float32)
             for s in range(SLOTS)], axis=0)
        scores = scores + bias
        top = jnp.max(scores, axis=0, keepdims=True)
        expo = jnp.exp(scores - top)
        prob = expo * (1.0 / jnp.sum(expo, axis=0, keepdims=True))
        centre = jnp.sum(prob * d_prob, axis=0, keepdims=True)
        d_score = prob * (d_prob - centre)
        mixed = jnp.concatenate([d_score.astype(jnp.bfloat16), prob.astype(jnp.bfloat16)], axis=1)
        rows = jnp.dot(keys_t, mixed, preferred_element_type=jnp.float32)
        d_query = rows[HD:, :BLOCK] * 0.125
        both_t = jnp.concatenate([rows[:HD, BLOCK:], d_query], axis=0)
        t1[b] = jnp.transpose(both_t).astype(jnp.bfloat16)
        left[b, 0:HD] = d_query.astype(jnp.bfloat16)
        terms[b] = jnp.dot(mixed, qc, preferred_element_type=jnp.float32).reshape(SLOTS, BLOCK, 128)

    def served(d):
        return lax.rem(me + half * d + (1 - half) * (ways - d), ways)

    def z_copy(d, src, dst, k):
        dest = served(d)
        return remote(src.at[dest], dst.at[head], z_send.at[k, d], z_recv.at[k, head], (node, dest))

    def step(k):
        @pl.when(k > 0)
        def _():
            source = lax.rem(me + ways - k, ways)
            remote(packed.at[0], landed.at[source], c_send.at[k], c_recv.at[k], around(k)).wait_recv()

        d = ways - 1 - k
        remote(packed.at[0], landed.at[lax.rem(me + k + 1, ways)], c_send.at[d], c_recv.at[d], around(d)).wait_recv()
        block(lax.rem(me + ways - k, ways))
        block(lax.rem(me + k + 1, ways))
        d = k + half

        @pl.when(jnp.logical_and(d >= 1, d < reach))
        def _():
            z_copy(d, t1, r1_ref, 0).start()

        @pl.when(jnp.logical_and(k == 3, carries))
        def _():
            def landed_piece(d):
                t, rows, lanes = tile(node)
                source = lax.rem(me + ways - d, ways)
                remote(shard.at[t, rows, lanes], all_ref.at[source, t, rows, lanes], a_send.at[d], a_recv.at[d],
                       around(d)).wait()

            loop(1, ways, landed_piece)
            loop(1, nodes // CORES, lambda d: plane_copy(node, d).start())

    loop(0, reach, step)

    def add(r, carry):
        run, before = carry
        entry = plan[order + r]
        here = plan[entry]
        keep = jnp.where(here == before, 1.0, 0.0)
        run = run * keep + terms[entry // SLOTS, lax.rem(entry, SLOTS)]
        runs[r] = run
        return run, here

    lax.fori_loop(0, ways * SLOTS, add, (jnp.zeros((BLOCK, 128), jnp.float32), jnp.int32(-1)), unroll=4)

    def total_of(c):
        total = runs[plan[last + c]]
        t2[c] = total.astype(jnp.bfloat16)
        left[c, HD:3 * HD] = jnp.transpose(total).astype(jnp.bfloat16)

    def total_and_send(j):
        d = reach - 1 - j
        total_of(served(d))
        z_copy(d, t2, r2_ref, 1).start()

    loop(0, reach - 1, total_and_send)
    total_of(me)
    loop(reach, ways, lambda d: total_of(served(d)))
    r1_ref[head] = t1[me]
    r2_ref[head] = t2[me]
    half_cols = HD // 2
    start = pl.multiple_of(half * half_cols, half_cols)
    for t in range(3):
        grads = jnp.concatenate([left[b, pl.ds(t * HD + start, half_cols), :] for b in range(ways)], axis=1)
        gw[t * half_cols:(t + 1) * half_cols, :] = jnp.dot(grads, feats[...], preferred_element_type=jnp.float32)

    def near_node(d):
        return (y * cross + lax.rem(near_me + d, cross), me)

    def y_node(d):
        return (lax.rem(y + d, ys) * cross + near_me, me)

    def piece(index):
        rows = 3 * cols // CORES
        return (pl.ds(pl.multiple_of(lax.rem(index, CORES) * rows, rows), rows),
                pl.ds(pl.multiple_of(index // CORES * 128, 128), 128))

    def near_copy(d):
        rows, lanes = piece(lax.rem(near_me + d, cross))
        return remote(gw.at[rows, lanes], near.at[d], n_send.at[d], n_recv.at[d], near_node(d))

    def y_copy(d):
        return remote(near.at[0], line.at[d], y_send.at[d], y_recv.at[d], y_node(d))

    my_rows, my_lanes = piece(near_me)

    def back_copy(d):
        return remote(line.at[0], out_ref.at[my_rows, my_lanes], g_send.at[d], g_recv.at[d], near_node(d))

    loop(1, cross, lambda d: near_copy(d).start())

    def end_plane(d):
        source = lax.rem(node + nodes - CORES * d, nodes)

        @pl.when(source // cross < 3)
        def _():
            plane_copy(source, d).wait_recv()

    loop(1, nodes // CORES, end_plane)
    core_copy(core).start()
    loop(1, cross, lambda d: near_copy(d).wait())
    total = gw[my_rows, my_lanes]
    for d in range(1, cross):
        total = total + near[d]
    near[0] = total
    loop(1, ys, lambda d: y_copy(d).start())
    loop(1, ys, lambda d: y_copy(d).wait())
    for d in range(1, ys):
        total = total + line[d]
    line[0] = total
    out_ref[my_rows, my_lanes] = total
    loop(1, cross, lambda d: back_copy(d).start())

    def end_back(d):
        back_copy(d).wait_send()
        rows, lanes = piece(lax.rem(near_me + cross - d, cross))
        remote(line.at[0], out_ref.at[rows, lanes], g_send.at[d], g_recv.at[d], near_node(d)).wait_recv()

    loop(1, cross, end_back)
    loop(1, ways, lambda d: cot_copy(d).wait_send())

    @pl.when(carries)
    def _():
        loop(1, nodes // CORES, lambda d: plane_copy(node, d).wait_send())

    core_copy(core).wait_send()
    core_copy(1 - core).wait_recv()

    def end_z(d):
        z_copy(d, t1, r1_ref, 0).wait_send()
        z_copy(d, t2, r2_ref, 1).wait_send()
        other = lax.rem(head + d, reach)
        remote(t1.at[0], r1_ref.at[other], z_send.at[0, d], z_recv.at[0, other], around(d)).wait_recv()
        remote(t2.at[0], r2_ref.at[other], z_send.at[1, d], z_recv.at[1, other], around(d)).wait_recv()

    loop(1, reach, end_z)


def finish_kernel(r1_ref, r2_ref, w_ref, gw_ref, attn_ref, gx_ref, gq_ref, gk_ref, gv_ref):
    low = low_lanes(BLOCK)
    for p in range(HEADS // 2):
        first = r1_ref[2 * p].astype(jnp.float32)
        second = pltpu.roll(r1_ref[2 * p + 1].astype(jnp.float32), 64, 1)
        attn_ref[:, 128 * p:128 * (p + 1)] = jnp.where(low, first, second).astype(jnp.bfloat16)
    total = jnp.zeros(gx_ref.shape, jnp.float32)
    zeros = jnp.zeros((HD, w_ref.shape[-1]), w_ref.dtype)
    for h in range(HEADS):
        wq = jnp.concatenate([zeros, w_ref[2 * h, 0], w_ref[2 * h + 1, 0]], axis=0)
        wvk = jnp.concatenate(
            [w_ref[2 * h, 1], w_ref[2 * h + 1, 1], w_ref[2 * h, 2], w_ref[2 * h + 1, 2]], axis=0)
        total = total + jnp.dot(r1_ref[h], wq, preferred_element_type=jnp.float32)
        total = total + jnp.dot(r2_ref[h], wvk, preferred_element_type=jnp.float32)
    gx_ref[...] = total.astype(jnp.bfloat16)
    cols = HD // 2
    gq_ref[...] = gw_ref[:cols]
    gv_ref[...] = gw_ref[cols:2 * cols]
    gk_ref[...] = gw_ref[2 * cols:]


def params(**kwargs):
    return pltpu.CompilerParams(vmem_limit_bytes=VMEM_BYTES, **kwargs)


def local(xs, ys, feats, cot, wq, wk, wv, adj, adj_count, perms):
    width = feats.shape[1]
    cols = wq.shape[1]
    group = feats.shape[0] // BLOCK
    ways = lax.axis_size("head")
    bf16, f32 = jnp.bfloat16, jnp.float32
    cross = xs * CORES
    nodes = xs * ys * CORES
    dma = pltpu.SemaphoreType.DMA
    sds = jax.ShapeDtypeStruct
    plan = pl.pallas_call(
        functools.partial(plan_kernel, group),
        out_shape=sds((2 * group * SLOTS + group,), jnp.int32),
        in_specs=[smem()] * 2,
        out_specs=smem(),
        scratch_shapes=[pltpu.SMEM((group,), jnp.int32)],
    )(adj.T, perms)
    r1, r2, weights, summed = pl.pallas_call(
        functools.partial(layer_kernel, ways, xs, ys),
        out_shape=(
            sds((HEADS, BLOCK, 128), bf16),
            sds((HEADS, BLOCK, 128), bf16),
            sds((ways, 3, cols, width), bf16),
            sds((3 * cols, width), f32),
        ),
        in_specs=[hbm()] * 7,
        out_specs=(vmem(),) * 4,
        scratch_shapes=[
            pltpu.SMEM((2 * group * SLOTS + group,), jnp.int32),
            pltpu.SMEM((group,), jnp.int32),
            pltpu.VMEM((BLOCK, width), bf16),
            pltpu.VMEM((group * BLOCK, width), bf16),
            pltpu.VMEM((3, cols, width), bf16),
            pltpu.VMEM((4, 2, cols, width), bf16),
            pltpu.VMEM((HEADS, 64, 128), bf16),
            pltpu.VMEM((ways, 64, 128), bf16),
            pltpu.VMEM((group, BLOCK, 128), bf16),
            pltpu.VMEM((group, 128, BLOCK), bf16),
            pltpu.VMEM((group, BLOCK, 128), bf16),
            pltpu.VMEM((group, SLOTS, BLOCK, 128), f32),
            pltpu.VMEM((group * SLOTS, BLOCK, 128), f32),
            pltpu.VMEM((group, BLOCK, 128), bf16),
            pltpu.VMEM((group, BLOCK, 128), bf16),
            pltpu.VMEM((group, 3 * HD, BLOCK), bf16),
            pltpu.VMEM((3 * cols, width), f32),
            pltpu.VMEM((cross, 3 * cols // CORES, 128), f32),
            pltpu.VMEM((ys, 3 * cols // CORES, 128), f32),
            dma((7,)), dma, dma, dma((ways,)), dma((ways,)), dma((ways,)), dma((ways,)),
            dma((nodes // CORES,)), dma((nodes // CORES,)), dma, dma,
            dma((2, ways // 2)), dma((2, ways // 2)), dma((cross,)), dma((cross,)),
            dma((ys,)), dma((ys,)), dma((cross,)), dma((cross,)),
        ],
        compiler_params=params(collective_id=0, has_side_effects=True),
        cost_estimate=pl.CostEstimate(flops=16 * 2 * 1024 * 256 * 384, bytes_accessed=8 << 20, transcendentals=1 << 21),
    )(plan, adj_count, wq.T, wv.T, wk.T, cot, feats)
    attn, grad_x, grad_wq, grad_wk, grad_wv = pl.pallas_call(
        finish_kernel,
        out_shape=(
            sds((BLOCK, width), bf16),
            sds((BLOCK, width), bf16),
            sds((cols, width), f32),
            sds((cols, width), f32),
            sds((cols, width), f32),
        ),
        in_specs=[vmem()] * 4,
        out_specs=(vmem(),) * 5,
        compiler_params=params(),
        cost_estimate=pl.CostEstimate(flops=2 * 128 * 2048 * 512, bytes_accessed=3 << 20, transcendentals=0),
    )(r1, r2, weights, summed)
    return (attn, grad_x, grad_wq.T, grad_wk.T, grad_wv.T)


def solution(mesh):
    nodes = mesh.shape["node"]
    xs = 4 if nodes >= 8 else nodes // CORES
    ys = nodes // (xs * CORES)
    return jax.shard_map(
        functools.partial(local, xs, ys),
        mesh=mesh,
        in_specs=(
            P("node", None),
            P(("node", "head"), None),
            P(None, "head"),
            P(None, "head"),
            P(None, "head"),
            P("node", None),
            P("node"),
            P(None, "node", None),
        ),
        out_specs=(
            P(("node", "head"), None),
            P(("node", "head"), None),
            P(None, "head"),
            P(None, "head"),
            P(None, "head"),
        ),
        check_vma=False,
    )
```

```python
import functools

import jax
import jax.numpy as jnp
from jax import lax
from jax.experimental import pallas as pl
from jax.experimental.pallas import tpu as pltpu
from jax.sharding import PartitionSpec as P

HEADS = 8
BLOCK = 128
MAXADJ = 4
MATCH = 3
SLOTS = 1 + MAXADJ + MATCH
HD = 64
CORES = 2
MESH = pl.DeviceIdType.MESH
VMEM_BYTES = 60 * 1024 * 1024
NT = (((1,), (1,)), ((), ()))


def vmem():
    return pl.BlockSpec(memory_space=pltpu.VMEM)


def hbm():
    return pl.BlockSpec(memory_space=pltpu.HBM)


def smem():
    return pl.BlockSpec(memory_space=pltpu.SMEM)


def low_lanes(rows):
    return lax.broadcasted_iota(jnp.int32, (rows, 128), 1) < HD


def flat(rows, at):
    return pltpu.roll(jnp.concatenate([rows, jnp.zeros((1, 128 - rows.shape[1]), jnp.int32)], axis=1), 16 * at, 1)


def make_plan(adj, perms, plan):
    lane = lax.broadcasted_iota(jnp.int32, (1, 128), 1)
    ids = jnp.where(lane < 16, lane, 0)
    for s in range(MAXADJ):
        ids = ids + flat(adj[s:s + 1, :], 1 + s)
    for m in range(MATCH):
        ids = ids + flat(perms[m], 1 + MAXADJ + m)
    across = lax.broadcasted_iota(jnp.int32, (128, 128), 1)
    down = lax.broadcasted_iota(jnp.int32, (128, 128), 0)

    def column(row):
        return jnp.sum(jnp.where(across == down, jnp.broadcast_to(row, (128, 128)), 0), axis=1, keepdims=True)

    ids_down = column(ids)
    before = ids_down * 128 + down < jnp.broadcast_to(ids * 128 + lane, (128, 128))
    rank = jnp.sum(jnp.where(before, 1, 0), axis=0, keepdims=True)
    order = jnp.sum(jnp.where(column(rank) == across, down, 0), axis=0, keepdims=True)
    last = jnp.sum(jnp.where(ids_down <= across, 1, 0), axis=0, keepdims=True) - 1
    plan[0:1, :] = ids
    plan[1:2, :] = order
    plan[2:3, :] = last
    plan[3:8, :] = jnp.zeros((5, 128), jnp.int32)


def loop(first, stop, act):
    def body(d, carry):
        act(d)
        return carry

    lax.fori_loop(first, stop, body, 0)


def layer_kernel(ways, xs, ys, adj_hbm, perms_hbm, counts_hbm, wq_hbm, wv_hbm, wk_hbm, cot_hbm, feats_hbm,
                 attn_ref, gx_ref, out_ref,
                 plan, counts, adj, perms, plan_rows, cot, feats, shard, wb, packed, landed, kv, kvt, qs, terms, runs, t1, t2, feats_t, gw,
                 near, line, r1_ref, r2_ref, all_ref, in_sem, w_send, w_recv, c_send, c_recv, f_send, f_recv, a_send, a_recv, p_send, p_recv, h_send, h_recv,
                 z_send, z_recv, n_send, n_recv, y_send, y_recv, g_send, g_recv):
    node = lax.axis_index("node")
    me = lax.axis_index("head")
    half = lax.rem(me, 2)
    head = me // 2
    partner = me + 1 - 2 * half
    cross = xs * CORES
    nodes = ys * cross
    y = node // cross
    near_me = lax.rem(node, cross)
    core = lax.rem(node, CORES)
    cols, width = wq_hbm.shape
    reach = ways // 2
    barrier = pltpu.get_barrier_semaphore()

    def around(d):
        return (node, lax.rem(me + d, ways))

    def across(d):
        return (lax.rem(node + d, nodes), me)

    def remote(src, dst, send_sem, recv_sem, device):
        return pltpu.make_async_remote_copy(
            src_ref=src, dst_ref=dst, send_sem=send_sem, recv_sem=recv_sem, device_id=device, device_id_type=MESH)

    loop(1, ways, lambda d: pl.semaphore_signal(barrier, inc=1, device_id=around(d), device_id_type=MESH))
    loop(1, nodes // CORES, lambda d: pl.semaphore_signal(
        barrier, inc=1, device_id=across(CORES * d), device_id_type=MESH))
    for x in range(xs):
        other = y * cross + lax.rem(near_me // CORES + x, xs) * CORES + 1 - core
        pl.semaphore_signal(barrier, inc=1, device_id=(other, me), device_id_type=MESH)
    inputs = [
        pltpu.make_async_copy(src, dst, in_sem.at[i])
        for i, (src, dst) in enumerate((
            (wq_hbm, shard.at[0]), (wv_hbm, shard.at[1]), (wk_hbm, shard.at[2]), (cot_hbm, cot),
            (feats_hbm, feats), (adj_hbm, adj), (perms_hbm, perms), (counts_hbm, counts)))
    ]
    for copy in inputs:
        copy.start()
    for copy in inputs[:4]:
        copy.wait()
    wb[0] = jnp.zeros(wb.shape[1:], wb.dtype)
    wb[pl.ds(1, 3), half] = shard[...]
    low = low_lanes(64)
    for p in range(HEADS // 2):
        pair = cot[:, 128 * p:128 * (p + 1)].astype(jnp.float32)
        first, second = pair[:64], pair[64:]
        packed[2 * p] = jnp.where(low, first, pltpu.roll(second, 64, 1)).astype(jnp.bfloat16)
        packed[2 * p + 1] = jnp.where(low, pltpu.roll(first, 64, 1), second).astype(jnp.bfloat16)
    landed[me] = packed[head]
    pl.semaphore_wait(barrier, (ways - 1) + (nodes // CORES - 1) + xs)

    w_copy = remote(shard, wb.at[pl.ds(1, 3), half], w_send, w_recv, (node, partner))
    w_copy.start()

    def served(d):
        return lax.rem(me + half * d + (1 - half) * (ways - d), ways)

    def passed(d):
        return lax.rem(partner + (1 - half) * d + half * (ways - d), ways)

    def cot_copy(d):
        down = lax.rem(me + d, 2)
        dest = lax.rem(me + (1 - down) * d + down * (ways - d), ways)
        return remote(packed.at[dest // 2], landed.at[me], c_send.at[d], c_recv.at[d], (node, dest))

    def pass_copy(d):
        block = served(d)
        return remote(landed.at[block], landed.at[block], f_send.at[d], f_recv.at[d], (node, partner))

    def tile(n):
        x = lax.rem(n // CORES, xs)
        core = lax.rem(n, CORES)
        rows = cols // CORES
        return (n // cross, pl.ds(pl.multiple_of(core * rows, rows), rows), pl.ds(pl.multiple_of(x * 128, 128), 128))

    def shard_copy(d):
        t, rows, lanes = tile(node)
        return remote(shard.at[t, rows, lanes], all_ref.at[me, t, rows, lanes], a_send.at[d], a_recv.at[d], around(d))

    def plane_copy(n, d):
        t, rows, lanes = tile(n)
        piece = all_ref.at[:, t, rows, lanes]
        return remote(piece, piece, p_send.at[d], p_recv.at[d], across(CORES * d))

    def core_copy(c):
        rows = pl.ds(pl.multiple_of(c * (cols // CORES), cols // CORES), cols // CORES)
        piece = all_ref.at[:, :, rows, :]
        return remote(piece, piece, h_send, h_recv, (node + 1 - 2 * core, me))

    carries = y < 3

    loop(1, reach, lambda d: cot_copy(d).start())
    pass_copy(0).start()

    @pl.when(carries)
    def _():
        t, rows, lanes = tile(node)
        all_ref[me, t, rows, lanes] = shard[t, rows, lanes]
        loop(1, ways, lambda d: shard_copy(d).start())

    for copy in inputs[4:]:
        copy.wait()
    make_plan(adj, perms, plan_rows)
    plan_copy = pltpu.make_async_copy(plan_rows, plan, in_sem.at[8])
    plan_copy.start()
    for b in range(ways):
        feats_t[:, b * BLOCK:(b + 1) * BLOCK] = jnp.transpose(feats[b * BLOCK:(b + 1) * BLOCK, :])
    plan_copy.wait()
    w_copy.wait()
    weights = wb[...].reshape(4 * HD, width)
    per = 4
    for c in range(ways // per):
        rows = feats[c * per * BLOCK:(c + 1) * per * BLOCK, :]
        out = lax.dot_general(rows, weights, NT, preferred_element_type=jnp.float32)
        for j in range(per):
            b = c * per + j
            part = out[j * BLOCK:(j + 1) * BLOCK]
            qs[b] = (part[:, :128].astype(jnp.bfloat16).astype(jnp.float32) * 0.125).astype(jnp.bfloat16)
            kv[b] = part[:, 128:].astype(jnp.bfloat16)
            kvt[b] = jnp.transpose(part[:, 128:]).astype(jnp.bfloat16)

    def block(b):
        ids = [plan[0, s * ways + b] for s in range(SLOTS)]
        count = counts[b]
        keys = jnp.concatenate([kv[i] for i in ids], axis=0)
        keys_t = jnp.concatenate([kvt[i] for i in ids], axis=1)
        got = landed[b].astype(jnp.float32)
        cot_rows = jnp.concatenate(
            [jnp.where(low, got, 0.0), jnp.where(low, pltpu.roll(got, 64, 1), 0.0)], axis=0).astype(jnp.bfloat16)
        qc = jnp.concatenate([qs[b], cot_rows], axis=0)
        both = lax.dot_general(keys, qc, NT, preferred_element_type=jnp.float32)
        scores = both[:, :BLOCK]
        d_prob = both[:, BLOCK:]
        bias = jnp.concatenate(
            [jnp.full((BLOCK, 1), jnp.where(s <= count, 0.0, -1e30) if 1 <= s <= MAXADJ else 0.0, jnp.float32)
             for s in range(SLOTS)], axis=0)
        scores = scores + bias
        top = jnp.max(scores, axis=0, keepdims=True)
        expo = jnp.exp(scores - top)
        prob = expo * (1.0 / jnp.sum(expo, axis=0, keepdims=True))
        centre = jnp.sum(prob * d_prob, axis=0, keepdims=True)
        d_score = prob * (d_prob - centre)
        mixed = jnp.concatenate([d_score.astype(jnp.bfloat16), prob.astype(jnp.bfloat16)], axis=1)
        rows = jnp.dot(keys_t, mixed, preferred_element_type=jnp.float32)
        d_query = rows[HD:, :BLOCK] * 0.125
        both_t = jnp.concatenate([rows[:HD, BLOCK:], d_query], axis=0)
        t1[b] = jnp.transpose(both_t).astype(jnp.bfloat16)
        terms[b] = jnp.dot(mixed, qc, preferred_element_type=jnp.float32).reshape(SLOTS, BLOCK, 128)

    def z_copy(d, src, dst, k):
        dest = served(d)
        return remote(src.at[dest], dst.at[head], z_send.at[k, d], z_recv.at[k, head], (node, dest))

    def arrive(d):
        source = served(d)
        remote(packed.at[0], landed.at[source], c_send.at[d], c_recv.at[d], (node, source)).wait_recv()
        pass_copy(d).start()

    def direct(k):
        @pl.when(k > 0)
        def _():
            arrive(2 * k)

        arrive(2 * k + 1)
        block(served(2 * k))
        block(served(2 * k + 1))

        @pl.when(k > 0)
        def _():
            z_copy(2 * k, t1, r1_ref, 0).start()

        z_copy(2 * k + 1, t1, r1_ref, 0).start()

    def second(k):
        for d in (2 * k, 2 * k + 1):
            other = landed.at[passed(d)]
            remote(other, other, f_send.at[d], f_recv.at[d], (node, partner)).wait_recv()
        block(passed(2 * k))
        block(passed(2 * k + 1))

    loop(0, reach // 2, direct)

    @pl.when(carries)
    def _():
        def landed_piece(d):
            t, rows, lanes = tile(node)
            source = lax.rem(me + ways - d, ways)
            remote(shard.at[t, rows, lanes], all_ref.at[source, t, rows, lanes], a_send.at[d], a_recv.at[d],
                   around(d)).wait()

        loop(1, ways, landed_piece)
        loop(1, nodes // CORES, lambda d: plane_copy(node, d).start())

    loop(0, reach // 2, second)

    def add(r, carry):
        run, before = carry
        entry = plan[1, r]
        here = plan[0, entry]
        keep = jnp.where(here == before, 1.0, 0.0)
        run = run * keep + terms[lax.rem(entry, ways), entry // ways]
        runs[r] = run
        return run, here

    lax.fori_loop(0, ways * SLOTS, add, (jnp.zeros((BLOCK, 128), jnp.float32), jnp.int32(-1)), unroll=8)

    def total_of(c):
        t2[c] = runs[plan[2, c]].astype(jnp.bfloat16)

    def total_and_send(j):
        d = reach - 1 - j
        total_of(served(d))
        z_copy(d, t2, r2_ref, 1).start()

    loop(0, reach - 1, total_and_send)
    total_of(me)
    for d in range(reach, ways):
        total_of(served(d))
    r1_ref[head] = t1[me]
    r2_ref[head] = t2[me]
    rows_all = ways * BLOCK
    grads = jnp.concatenate([t1[...].reshape(rows_all, 128), t2[...].reshape(rows_all, 128)], axis=1)
    outer = jnp.dot(feats_t[...], grads, preferred_element_type=jnp.float32)
    one, two = outer[:, :128], outer[:, 128:]
    lane = lax.broadcasted_iota(jnp.int32, one.shape, 1)
    first_half = half == 0
    q_part = jnp.where(first_half, pltpu.roll(one, 64, 1), pltpu.roll(one, 32, 1))
    v_part = jnp.where(first_half, pltpu.roll(two, 32, 1), two)
    k_part = jnp.where(first_half, two, pltpu.roll(two, 96, 1))
    gw[...] = jnp.transpose(jnp.where(lane < 32, q_part, jnp.where(lane < 64, v_part, k_part)))[:3 * cols]

    def near_node(d):
        return (y * cross + lax.rem(near_me + d, cross), me)

    def y_node(d):
        return (lax.rem(y + d, ys) * cross + near_me, me)

    def piece(index):
        rows = 3 * cols // CORES
        return (pl.ds(pl.multiple_of(lax.rem(index, CORES) * rows, rows), rows),
                pl.ds(pl.multiple_of(index // CORES * 128, 128), 128))

    def near_copy(d):
        rows, lanes = piece(lax.rem(near_me + d, cross))
        return remote(gw.at[rows, lanes], near.at[d], n_send.at[d], n_recv.at[d], near_node(d))

    def y_copy(d):
        return remote(near.at[0], line.at[d], y_send.at[d], y_recv.at[d], y_node(d))

    my_rows, my_lanes = piece(near_me)

    def back_copy(d):
        return remote(line.at[0], out_ref.at[my_rows, my_lanes], g_send.at[d], g_recv.at[d], near_node(d))

    loop(1, cross, lambda d: near_copy(d).start())

    def end_plane(d):
        source = lax.rem(node + nodes - CORES * d, nodes)

        @pl.when(source // cross < 3)
        def _():
            plane_copy(source, d).wait_recv()

    loop(1, nodes // CORES, end_plane)
    core_copy(core).start()
    loop(1, cross, lambda d: near_copy(d).wait())
    total = gw[my_rows, my_lanes]
    for d in range(1, cross):
        total = total + near[d]
    near[0] = total
    loop(1, ys, lambda d: y_copy(d).start())

    def end_first(d):
        z_copy(d, t1, r1_ref, 0).wait_send()
        other = lax.rem(head + d, reach)
        remote(t1.at[0], r1_ref.at[other], z_send.at[0, d], z_recv.at[0, other], around(d)).wait_recv()

    loop(1, reach, end_first)
    low_all = low_lanes(BLOCK)
    for p in range(HEADS // 2):
        first = r1_ref[2 * p].astype(jnp.float32)
        second_head = pltpu.roll(r1_ref[2 * p + 1].astype(jnp.float32), 64, 1)
        attn_ref[:, 128 * p:128 * (p + 1)] = jnp.where(low_all, first, second_head).astype(jnp.bfloat16)
    loop(1, ys, lambda d: y_copy(d).wait())
    for d in range(1, ys):
        total = total + line[d]
    line[0] = total
    out_ref[my_rows, my_lanes] = total
    loop(1, cross, lambda d: back_copy(d).start())

    core_copy(core).wait_send()
    core_copy(1 - core).wait_recv()
    grad = jnp.zeros(gx_ref.shape, jnp.float32)
    zeros = jnp.zeros((HD, width), jnp.bfloat16)
    for h in range(HEADS):
        wq = jnp.concatenate([zeros, all_ref[2 * h, 0], all_ref[2 * h + 1, 0]], axis=0)
        grad = grad + jnp.dot(r1_ref[h], wq, preferred_element_type=jnp.float32)

    def end_last(d):
        z_copy(d, t2, r2_ref, 1).wait_send()
        other = lax.rem(head + d, reach)
        remote(t2.at[0], r2_ref.at[other], z_send.at[1, d], z_recv.at[1, other], around(d)).wait_recv()

    loop(1, reach, end_last)
    for h in range(HEADS):
        wvk = jnp.concatenate(
            [all_ref[2 * h, 1], all_ref[2 * h + 1, 1], all_ref[2 * h, 2], all_ref[2 * h + 1, 2]], axis=0)
        grad = grad + jnp.dot(r2_ref[h], wvk, preferred_element_type=jnp.float32)
    gx_ref[...] = grad.astype(jnp.bfloat16)

    def end_back(d):
        back_copy(d).wait_send()
        rows, lanes = piece(lax.rem(near_me + cross - d, cross))
        remote(line.at[0], out_ref.at[rows, lanes], g_send.at[d], g_recv.at[d], near_node(d)).wait_recv()

    loop(1, cross, end_back)
    loop(1, reach, lambda d: cot_copy(d).wait_send())
    loop(0, reach, lambda d: pass_copy(d).wait_send())

    @pl.when(carries)
    def _():
        loop(1, nodes // CORES, lambda d: plane_copy(node, d).wait_send())


def finish_kernel(attn_in, gx_in, gw_ref, attn_ref, gx_ref, gq_ref, gk_ref, gv_ref):
    cols = HD // 2
    attn_ref[...] = attn_in[...]
    gx_ref[...] = gx_in[...]
    gq_ref[...] = gw_ref[:cols]
    gv_ref[...] = gw_ref[cols:2 * cols]
    gk_ref[...] = gw_ref[2 * cols:]


def params(**kwargs):
    return pltpu.CompilerParams(vmem_limit_bytes=VMEM_BYTES, **kwargs)


def local(xs, ys, feats, cot, wq, wk, wv, adj, adj_count, perms):
    width = feats.shape[1]
    cols = wq.shape[1]
    group = feats.shape[0] // BLOCK
    ways = lax.axis_size("head")
    bf16, f32 = jnp.bfloat16, jnp.float32
    cross = xs * CORES
    nodes = xs * ys * CORES
    dma = pltpu.SemaphoreType.DMA
    sds = jax.ShapeDtypeStruct
    attn, grad_x, summed = pl.pallas_call(
        functools.partial(layer_kernel, ways, xs, ys),
        out_shape=(sds((BLOCK, width), bf16), sds((BLOCK, width), bf16), sds((3 * cols, width), f32)),
        in_specs=[hbm()] * 8,
        out_specs=(vmem(),) * 3,
        scratch_shapes=[
            pltpu.SMEM((8, 128), jnp.int32),
            pltpu.SMEM((group,), jnp.int32),
            pltpu.VMEM((MAXADJ, group), jnp.int32),
            pltpu.VMEM((MATCH, 1, group), jnp.int32),
            pltpu.VMEM((8, 128), jnp.int32),
            pltpu.VMEM((BLOCK, width), bf16),
            pltpu.VMEM((group * BLOCK, width), bf16),
            pltpu.VMEM((3, cols, width), bf16),
            pltpu.VMEM((4, 2, cols, width), bf16),
            pltpu.VMEM((HEADS, 64, 128), bf16),
            pltpu.VMEM((ways, 64, 128), bf16),
            pltpu.VMEM((group, BLOCK, 128), bf16),
            pltpu.VMEM((group, 128, BLOCK), bf16),
            pltpu.VMEM((group, BLOCK, 128), bf16),
            pltpu.VMEM((group, SLOTS, BLOCK, 128), f32),
            pltpu.VMEM((group * SLOTS, BLOCK, 128), f32),
            pltpu.VMEM((group, BLOCK, 128), bf16),
            pltpu.VMEM((group, BLOCK, 128), bf16),
            pltpu.VMEM((width, group * BLOCK), bf16),
            pltpu.VMEM((3 * cols, width), f32),
            pltpu.VMEM((cross, 3 * cols // CORES, 128), f32),
            pltpu.VMEM((ys, 3 * cols // CORES, 128), f32),
            pltpu.VMEM((HEADS, BLOCK, 128), bf16),
            pltpu.VMEM((HEADS, BLOCK, 128), bf16),
            pltpu.VMEM((ways, 3, cols, width), bf16),
            dma((9,)), dma, dma, dma((ways // 2,)), dma((ways // 2,)), dma((ways // 2,)), dma((ways // 2,)), dma((ways,)), dma((ways,)),
            dma((nodes // CORES,)), dma((nodes // CORES,)), dma, dma,
            dma((2, ways // 2)), dma((2, ways // 2)), dma((cross,)), dma((cross,)),
            dma((ys,)), dma((ys,)), dma((cross,)), dma((cross,)),
        ],
        compiler_params=params(collective_id=0, has_side_effects=True),
        cost_estimate=pl.CostEstimate(flops=16 * 2 * 1024 * 256 * 384, bytes_accessed=8 << 20, transcendentals=1 << 21),
    )(adj.T, perms, adj_count, wq.T, wv.T, wk.T, cot, feats)
    attn, grad_x, grad_wq, grad_wk, grad_wv = pl.pallas_call(
        finish_kernel,
        out_shape=(
            sds((BLOCK, width), bf16),
            sds((BLOCK, width), bf16),
            sds((cols, width), f32),
            sds((cols, width), f32),
            sds((cols, width), f32),
        ),
        in_specs=[vmem()] * 3,
        out_specs=(vmem(),) * 5,
        compiler_params=params(),
        cost_estimate=pl.CostEstimate(flops=0, bytes_accessed=1 << 20, transcendentals=0),
    )(attn, grad_x, summed)
    return (attn, grad_x, grad_wq.T, grad_wk.T, grad_wv.T)


def solution(mesh):
    nodes = mesh.shape["node"]
    xs = 4 if nodes >= 8 else nodes // CORES
    ys = nodes // (xs * CORES)
    return jax.shard_map(
        functools.partial(local, xs, ys),
        mesh=mesh,
        in_specs=(
            P("node", None),
            P(("node", "head"), None),
            P(None, "head"),
            P(None, "head"),
            P(None, "head"),
            P("node", None),
            P("node"),
            P(None, "node", None),
        ),
        out_specs=(
            P(("node", "head"), None),
            P(("node", "head"), None),
            P(None, "head"),
            P(None, "head"),
            P(None, "head"),
        ),
        check_vma=False,
    )
```

```python
import functools

import jax
import jax.numpy as jnp
from jax import lax
from jax.experimental import pallas as pl
from jax.experimental.pallas import tpu as pltpu
from jax.sharding import PartitionSpec as P

HEADS = 8
BLOCK = 128
MAXADJ = 4
MATCH = 3
SLOTS = 1 + MAXADJ + MATCH
HD = 64
CORES = 2
MESH = pl.DeviceIdType.MESH
VMEM_BYTES = 60 * 1024 * 1024
NT = (((1,), (1,)), ((), ()))


def vmem():
    return pl.BlockSpec(memory_space=pltpu.VMEM)


def hbm():
    return pl.BlockSpec(memory_space=pltpu.HBM)


def smem():
    return pl.BlockSpec(memory_space=pltpu.SMEM)


def low_lanes(rows):
    return lax.broadcasted_iota(jnp.int32, (rows, 128), 1) < HD


def flat(rows, at):
    return pltpu.roll(jnp.concatenate([rows, jnp.zeros((1, 128 - rows.shape[1]), jnp.int32)], axis=1), 16 * at, 1)


def make_plan(adj, perms, plan):
    lane = lax.broadcasted_iota(jnp.int32, (1, 128), 1)
    ids = jnp.where(lane < 16, lane, 0)
    for s in range(MAXADJ):
        ids = ids + flat(adj[s:s + 1, :], 1 + s)
    for m in range(MATCH):
        ids = ids + flat(perms[m], 1 + MAXADJ + m)
    across = lax.broadcasted_iota(jnp.int32, (128, 128), 1)
    down = lax.broadcasted_iota(jnp.int32, (128, 128), 0)

    def column(row):
        return jnp.sum(jnp.where(across == down, jnp.broadcast_to(row, (128, 128)), 0), axis=1, keepdims=True)

    ids_down = column(ids)
    before = ids_down * 128 + down < jnp.broadcast_to(ids * 128 + lane, (128, 128))
    rank = jnp.sum(jnp.where(before, 1, 0), axis=0, keepdims=True)
    order = jnp.sum(jnp.where(column(rank) == across, down, 0), axis=0, keepdims=True)
    last = jnp.sum(jnp.where(ids_down <= across, 1, 0), axis=0, keepdims=True) - 1
    plan[0:1, :] = ids
    plan[1:2, :] = order
    plan[2:3, :] = last
    plan[3:8, :] = jnp.zeros((5, 128), jnp.int32)


def loop(first, stop, act):
    def body(d, carry):
        act(d)
        return carry

    lax.fori_loop(first, stop, body, 0)


def layer_kernel(ways, xs, ys, adj_hbm, perms_hbm, counts_hbm, wq_hbm, wv_hbm, wk_hbm, cot_hbm, feats_hbm,
                 attn_ref, gx_ref, out_ref,
                 plan, counts, adj, perms, plan_rows, cot, feats, shard, wb, packed, landed, kv, kvt, qs, terms, runs, t1, t2, feats_t, gw,
                 near, line, r1_ref, r2_ref, all_ref, in_sem, w_send, w_recv, c_send, c_recv, f_send, f_recv, a_send, a_recv, p_send, p_recv, h_send, h_recv,
                 z_send, z_recv, n_send, n_recv, y_send, y_recv, g_send, g_recv):
    node = lax.axis_index("node")
    me = lax.axis_index("head")
    half = lax.rem(me, 2)
    head = me // 2
    partner = me + 1 - 2 * half
    cross = xs * CORES
    nodes = ys * cross
    y = node // cross
    near_me = lax.rem(node, cross)
    core = lax.rem(node, CORES)
    cols, width = wq_hbm.shape
    reach = ways // 2
    barrier = pltpu.get_barrier_semaphore()

    def around(d):
        return (node, lax.rem(me + d, ways))

    def across(d):
        return (lax.rem(node + d, nodes), me)

    def remote(src, dst, send_sem, recv_sem, device):
        return pltpu.make_async_remote_copy(
            src_ref=src, dst_ref=dst, send_sem=send_sem, recv_sem=recv_sem, device_id=device, device_id_type=MESH)

    loop(1, ways, lambda d: pl.semaphore_signal(barrier, inc=1, device_id=around(d), device_id_type=MESH))
    loop(1, nodes // CORES, lambda d: pl.semaphore_signal(
        barrier, inc=1, device_id=across(CORES * d), device_id_type=MESH))
    for x in range(xs):
        other = y * cross + lax.rem(near_me // CORES + x, xs) * CORES + 1 - core
        pl.semaphore_signal(barrier, inc=1, device_id=(other, me), device_id_type=MESH)
    inputs = [
        pltpu.make_async_copy(src, dst, in_sem.at[i])
        for i, (src, dst) in enumerate((
            (wq_hbm, shard.at[0]), (wv_hbm, shard.at[1]), (wk_hbm, shard.at[2]), (cot_hbm, cot),
            (feats_hbm, feats), (adj_hbm, adj), (perms_hbm, perms), (counts_hbm, counts)))
    ]
    for copy in inputs:
        copy.start()
    for copy in inputs[:4]:
        copy.wait()
    wb[0] = jnp.zeros(wb.shape[1:], wb.dtype)
    wb[pl.ds(1, 3), half] = shard[...]
    low = low_lanes(64)
    for p in range(HEADS // 2):
        pair = cot[:, 128 * p:128 * (p + 1)].astype(jnp.float32)
        first, second = pair[:64], pair[64:]
        packed[2 * p] = jnp.where(low, first, pltpu.roll(second, 64, 1)).astype(jnp.bfloat16)
        packed[2 * p + 1] = jnp.where(low, pltpu.roll(first, 64, 1), second).astype(jnp.bfloat16)
    landed[me] = packed[head]
    for copy in inputs[4:]:
        copy.wait()
    make_plan(adj, perms, plan_rows)
    plan_copy = pltpu.make_async_copy(plan_rows, plan, in_sem.at[8])
    plan_copy.start()
    for b in range(ways):
        feats_t[:, b * BLOCK:(b + 1) * BLOCK] = jnp.transpose(feats[b * BLOCK:(b + 1) * BLOCK, :])
    pl.semaphore_wait(barrier, (ways - 1) + (nodes // CORES - 1) + xs)

    w_copy = remote(shard, wb.at[pl.ds(1, 3), half], w_send, w_recv, (node, partner))
    w_copy.start()

    def served(d):
        return lax.rem(me + half * d + (1 - half) * (ways - d), ways)

    def passed(d):
        return lax.rem(partner + (1 - half) * d + half * (ways - d), ways)

    def cot_copy(d):
        down = lax.rem(me + d, 2)
        dest = lax.rem(me + (1 - down) * d + down * (ways - d), ways)
        return remote(packed.at[dest // 2], landed.at[me], c_send, c_recv.at[d], (node, dest))

    def pass_copy(d):
        block = served(d)
        return remote(landed.at[block], landed.at[block], f_send, f_recv.at[d], (node, partner))

    def tile(n):
        x = lax.rem(n // CORES, xs)
        core = lax.rem(n, CORES)
        rows = cols // CORES
        return (n // cross, pl.ds(pl.multiple_of(core * rows, rows), rows), pl.ds(pl.multiple_of(x * 128, 128), 128))

    def shard_copy(d):
        t, rows, lanes = tile(node)
        return remote(shard.at[t, rows, lanes], all_ref.at[me, t, rows, lanes], a_send, a_recv, around(d))

    def plane_copy(n, d):
        t, rows, lanes = tile(n)
        piece = all_ref.at[:, t, rows, lanes]
        return remote(piece, piece, p_send, p_recv, across(CORES * d))

    def core_copy(c):
        rows = pl.ds(pl.multiple_of(c * (cols // CORES), cols // CORES), cols // CORES)
        piece = all_ref.at[:, :, rows, :]
        return remote(piece, piece, h_send, h_recv, (node + 1 - 2 * core, me))

    carries = y < 3

    def all_bytes(rows, send_sem, recv_sem):
        return remote(rows, rows, send_sem, recv_sem, (node, partner))

    @pl.when(carries)
    def _():
        t, rows, lanes = tile(node)
        all_ref[me, t, rows, lanes] = shard[t, rows, lanes]
        loop(1, ways, lambda d: shard_copy(d).start())

    loop(1, reach, lambda d: cot_copy(d).start())
    pass_copy(0).start()

    plan_copy.wait()
    w_copy.wait()
    weights = wb[...].reshape(4 * HD, width)
    per = 4
    for c in range(ways // per):
        rows = feats[c * per * BLOCK:(c + 1) * per * BLOCK, :]
        out = lax.dot_general(rows, weights, NT, preferred_element_type=jnp.float32)
        for j in range(per):
            b = c * per + j
            part = out[j * BLOCK:(j + 1) * BLOCK]
            qs[b] = (part[:, :128].astype(jnp.bfloat16).astype(jnp.float32) * 0.125).astype(jnp.bfloat16)
            kv[b] = part[:, 128:].astype(jnp.bfloat16)
            kvt[b] = jnp.transpose(part[:, 128:]).astype(jnp.bfloat16)

    def block(b):
        ids = [plan[0, s * ways + b] for s in range(SLOTS)]
        count = counts[b]
        keys = jnp.concatenate([kv[i] for i in ids], axis=0)
        keys_t = jnp.concatenate([kvt[i] for i in ids], axis=1)
        got = landed[b].astype(jnp.float32)
        cot_rows = jnp.concatenate(
            [jnp.where(low, got, 0.0), jnp.where(low, pltpu.roll(got, 64, 1), 0.0)], axis=0).astype(jnp.bfloat16)
        qc = jnp.concatenate([qs[b], cot_rows], axis=0)
        both = lax.dot_general(keys, qc, NT, preferred_element_type=jnp.float32)
        d_prob = both[:, BLOCK:]
        scores = []
        for s in range(SLOTS):
            part = both[s * BLOCK:(s + 1) * BLOCK, :BLOCK]
            scores.append(part + jnp.where(s <= count, 0.0, -1e30) if 1 <= s <= MAXADJ else part)
        scores = jnp.concatenate(scores, axis=0)
        expo = jnp.exp(scores - jnp.max(scores, axis=0, keepdims=True))
        recip = 1.0 / jnp.sum(expo, axis=0, keepdims=True)
        centre = jnp.sum(expo * d_prob, axis=0, keepdims=True) * recip
        prob = expo * recip
        d_score = prob * (d_prob - centre)
        mixed = jnp.concatenate([d_score.astype(jnp.bfloat16), prob.astype(jnp.bfloat16)], axis=1)
        rows = jnp.dot(keys_t, mixed, preferred_element_type=jnp.float32)
        d_query = rows[HD:, :BLOCK] * 0.125
        both_t = jnp.concatenate([rows[:HD, BLOCK:], d_query], axis=0)
        t1[b] = jnp.transpose(both_t).astype(jnp.bfloat16)
        terms[b] = jnp.dot(mixed, qc, preferred_element_type=jnp.float32).reshape(SLOTS, BLOCK, 128)

    def z_copy(d, src, dst, k):
        dest = served(d)
        return remote(src.at[dest], dst.at[head], z_send.at[k], z_recv.at[k], (node, dest))

    def arrive(d):
        source = served(d)
        remote(packed.at[0], landed.at[source], c_send, c_recv.at[d], (node, source)).wait_recv()
        pass_copy(d).start()

    def direct(k):
        @pl.when(k > 0)
        def _():
            arrive(2 * k)

        arrive(2 * k + 1)
        block(served(2 * k))
        block(served(2 * k + 1))

        @pl.when(k > 0)
        def _():
            z_copy(2 * k, t1, r1_ref, 0).start()

        z_copy(2 * k + 1, t1, r1_ref, 0).start()

        @pl.when(jnp.logical_and(carries, k == 1))
        def _():
            t, rows, lanes = tile(node)
            pieces = all_ref.at[pl.ds(0, ways - 1), t, rows, lanes]
            all_bytes(pieces, a_send, a_recv).wait()
            loop(1, nodes // CORES, lambda d: plane_copy(node, d).start())

    def second(k):
        for d in (2 * k, 2 * k + 1):
            other = landed.at[passed(d)]
            remote(other, other, f_send, f_recv.at[d], (node, partner)).wait_recv()
        block(passed(2 * k))
        block(passed(2 * k + 1))

    loop(0, reach // 2, direct)

    loop(0, reach // 2, second)

    def add(r, carry):
        run, before = carry
        entry = plan[1, r]
        here = plan[0, entry]
        keep = jnp.where(here == before, 1.0, 0.0)
        run = run * keep + terms[lax.rem(entry, ways), entry // ways]
        runs[r] = run
        return run, here

    lax.fori_loop(0, ways * SLOTS, add, (jnp.zeros((BLOCK, 128), jnp.float32), jnp.int32(-1)), unroll=8)

    def total_of(c):
        t2[c] = runs[plan[2, c]].astype(jnp.bfloat16)

    def total_and_send(j):
        d = reach - 1 - j
        total_of(served(d))
        z_copy(d, t2, r2_ref, 1).start()

    loop(0, reach - 1, total_and_send)
    total_of(me)
    for d in range(reach, ways):
        total_of(served(d))
    r1_ref[head] = t1[me]
    r2_ref[head] = t2[me]
    rows_all = ways * BLOCK
    grads = jnp.concatenate([t1[...].reshape(rows_all, 128), t2[...].reshape(rows_all, 128)], axis=1)
    outer = jnp.dot(feats_t[...], grads, preferred_element_type=jnp.float32)
    one, two = outer[:, :128], outer[:, 128:]
    lane = lax.broadcasted_iota(jnp.int32, one.shape, 1)
    first_half = half == 0
    q_part = jnp.where(first_half, pltpu.roll(one, 64, 1), pltpu.roll(one, 32, 1))
    v_part = jnp.where(first_half, pltpu.roll(two, 32, 1), two)
    k_part = jnp.where(first_half, two, pltpu.roll(two, 96, 1))
    gw[...] = jnp.transpose(jnp.where(lane < 32, q_part, jnp.where(lane < 64, v_part, k_part)))[:3 * cols]

    def near_node(d):
        return (y * cross + lax.rem(near_me + d, cross), me)

    def y_node(d):
        return (lax.rem(y + d, ys) * cross + near_me, me)

    def piece(index):
        rows = 3 * cols // CORES
        return (pl.ds(pl.multiple_of(lax.rem(index, CORES) * rows, rows), rows),
                pl.ds(pl.multiple_of(index // CORES * 128, 128), 128))

    def near_copy(d):
        rows, lanes = piece(lax.rem(near_me + d, cross))
        return remote(gw.at[rows, lanes], near.at[d], n_send, n_recv, near_node(d))

    def y_copy(d):
        return remote(near.at[0], line.at[d], y_send, y_recv, y_node(d))

    my_rows, my_lanes = piece(near_me)

    def back_copy(d):
        return remote(line.at[0], out_ref.at[my_rows, my_lanes], g_send, g_recv, near_node(d))

    loop(1, cross, lambda d: near_copy(d).start())

    carriers = 3 * xs

    @pl.when(carries)
    def _():
        all_bytes(runs.at[pl.ds(0, carriers - 1)], p_send, p_recv).wait_recv()

    @pl.when(jnp.logical_not(carries))
    def _():
        all_bytes(runs.at[pl.ds(0, carriers)], p_send, p_recv).wait_recv()

    core_copy(core).start()
    all_bytes(near.at[pl.ds(0, cross - 1)], n_send, n_recv).wait()
    total = gw[my_rows, my_lanes]
    for d in range(1, cross):
        total = total + near[d]
    near[0] = total
    loop(1, ys, lambda d: y_copy(d).start())

    all_bytes(t1.at[pl.ds(0, reach - 1)], z_send.at[0], z_recv.at[0]).wait()
    low_all = low_lanes(BLOCK)
    for p in range(HEADS // 2):
        first = r1_ref[2 * p].astype(jnp.float32)
        second_head = pltpu.roll(r1_ref[2 * p + 1].astype(jnp.float32), 64, 1)
        attn_ref[:, 128 * p:128 * (p + 1)] = jnp.where(low_all, first, second_head).astype(jnp.bfloat16)
    all_bytes(line.at[pl.ds(0, ys - 1)], y_send, y_recv).wait()
    for d in range(1, ys):
        total = total + line[d]
    line[0] = total
    out_ref[my_rows, my_lanes] = total
    loop(1, cross, lambda d: back_copy(d).start())

    core_copy(core).wait_send()
    core_copy(1 - core).wait_recv()
    grad = jnp.zeros(gx_ref.shape, jnp.float32)
    zeros = jnp.zeros((HD, width), jnp.bfloat16)
    for h in range(HEADS):
        wq = jnp.concatenate([zeros, all_ref[2 * h, 0], all_ref[2 * h + 1, 0]], axis=0)
        grad = grad + jnp.dot(r1_ref[h], wq, preferred_element_type=jnp.float32)

    all_bytes(t2.at[pl.ds(0, reach - 1)], z_send.at[1], z_recv.at[1]).wait()
    for h in range(HEADS):
        wvk = jnp.concatenate(
            [all_ref[2 * h, 1], all_ref[2 * h + 1, 1], all_ref[2 * h, 2], all_ref[2 * h + 1, 2]], axis=0)
        grad = grad + jnp.dot(r2_ref[h], wvk, preferred_element_type=jnp.float32)
    gx_ref[...] = grad.astype(jnp.bfloat16)

    all_bytes(near.at[pl.ds(0, cross - 1)], g_send, g_recv).wait()
    all_bytes(landed.at[pl.ds(0, reach - 1)], c_send, c_send).wait_send()
    all_bytes(landed.at[pl.ds(0, reach)], f_send, f_send).wait_send()

    @pl.when(carries)
    def _():
        all_bytes(runs.at[pl.ds(0, nodes // CORES - 1)], p_send, p_recv).wait_send()


def finish_kernel(attn_in, gx_in, gw_ref, attn_ref, gx_ref, gq_ref, gk_ref, gv_ref):
    cols = HD // 2
    attn_ref[...] = attn_in[...]
    gx_ref[...] = gx_in[...]
    gq_ref[...] = gw_ref[:cols]
    gv_ref[...] = gw_ref[cols:2 * cols]
    gk_ref[...] = gw_ref[2 * cols:]


def params(**kwargs):
    return pltpu.CompilerParams(vmem_limit_bytes=VMEM_BYTES, **kwargs)


def local(xs, ys, feats, cot, wq, wk, wv, adj, adj_count, perms):
    width = feats.shape[1]
    cols = wq.shape[1]
    group = feats.shape[0] // BLOCK
    ways = lax.axis_size("head")
    bf16, f32 = jnp.bfloat16, jnp.float32
    cross = xs * CORES
    nodes = xs * ys * CORES
    dma = pltpu.SemaphoreType.DMA
    sds = jax.ShapeDtypeStruct
    attn, grad_x, summed = pl.pallas_call(
        functools.partial(layer_kernel, ways, xs, ys),
        out_shape=(sds((BLOCK, width), bf16), sds((BLOCK, width), bf16), sds((3 * cols, width), f32)),
        in_specs=[hbm()] * 8,
        out_specs=(vmem(),) * 3,
        scratch_shapes=[
            pltpu.SMEM((8, 128), jnp.int32),
            pltpu.SMEM((group,), jnp.int32),
            pltpu.VMEM((MAXADJ, group), jnp.int32),
            pltpu.VMEM((MATCH, 1, group), jnp.int32),
            pltpu.VMEM((8, 128), jnp.int32),
            pltpu.VMEM((BLOCK, width), bf16),
            pltpu.VMEM((group * BLOCK, width), bf16),
            pltpu.VMEM((3, cols, width), bf16),
            pltpu.VMEM((4, 2, cols, width), bf16),
            pltpu.VMEM((HEADS, 64, 128), bf16),
            pltpu.VMEM((ways, 64, 128), bf16),
            pltpu.VMEM((group, BLOCK, 128), bf16),
            pltpu.VMEM((group, 128, BLOCK), bf16),
            pltpu.VMEM((group, BLOCK, 128), bf16),
            pltpu.VMEM((group, SLOTS, BLOCK, 128), f32),
            pltpu.VMEM((group * SLOTS, BLOCK, 128), f32),
            pltpu.VMEM((group, BLOCK, 128), bf16),
            pltpu.VMEM((group, BLOCK, 128), bf16),
            pltpu.VMEM((width, group * BLOCK), bf16),
            pltpu.VMEM((3 * cols, width), f32),
            pltpu.VMEM((cross, 3 * cols // CORES, 128), f32),
            pltpu.VMEM((ys, 3 * cols // CORES, 128), f32),
            pltpu.VMEM((HEADS, BLOCK, 128), bf16),
            pltpu.VMEM((HEADS, BLOCK, 128), bf16),
            pltpu.VMEM((ways, 3, cols, width), bf16),
            dma((9,)), dma, dma, dma, dma((ways // 2,)), dma, dma((ways // 2,)), dma, dma, dma, dma, dma, dma,
            dma((2,)), dma((2,)), dma, dma, dma, dma, dma, dma,
        ],
        compiler_params=params(collective_id=0, has_side_effects=True),
        cost_estimate=pl.CostEstimate(flops=16 * 2 * 1024 * 256 * 384, bytes_accessed=8 << 20, transcendentals=1 << 21),
    )(adj.T, perms, adj_count, wq.T, wv.T, wk.T, cot, feats)
    attn, grad_x, grad_wq, grad_wk, grad_wv = pl.pallas_call(
        finish_kernel,
        out_shape=(
            sds((BLOCK, width), bf16),
            sds((BLOCK, width), bf16),
            sds((cols, width), f32),
            sds((cols, width), f32),
            sds((cols, width), f32),
        ),
        in_specs=[vmem()] * 3,
        out_specs=(vmem(),) * 5,
        compiler_params=params(),
        cost_estimate=pl.CostEstimate(flops=0, bytes_accessed=1 << 20, transcendentals=0),
    )(attn, grad_x, summed)
    return (attn, grad_x, grad_wq.T, grad_wk.T, grad_wv.T)


def solution(mesh):
    nodes = mesh.shape["node"]
    xs = 4 if nodes >= 8 else nodes // CORES
    ys = nodes // (xs * CORES)
    return jax.shard_map(
        functools.partial(local, xs, ys),
        mesh=mesh,
        in_specs=(
            P("node", None),
            P(("node", "head"), None),
            P(None, "head"),
            P(None, "head"),
            P(None, "head"),
            P("node", None),
            P("node"),
            P(None, "node", None),
        ),
        out_specs=(
            P(("node", "head"), None),
            P(("node", "head"), None),
            P(None, "head"),
            P(None, "head"),
            P(None, "head"),
        ),
        check_vma=False,
    )
```

```python
import functools

import jax
import jax.numpy as jnp
from jax import lax
from jax.experimental import pallas as pl
from jax.experimental.pallas import tpu as pltpu
from jax.sharding import PartitionSpec as P

HEADS = 8
BLOCK = 128
MAXADJ = 4
MATCH = 3
SLOTS = 1 + MAXADJ + MATCH
HD = 64
CORES = 2
MESH = pl.DeviceIdType.MESH
VMEM_BYTES = 60 * 1024 * 1024
NT = (((1,), (1,)), ((), ()))


def vmem():
    return pl.BlockSpec(memory_space=pltpu.VMEM)


def hbm():
    return pl.BlockSpec(memory_space=pltpu.HBM)


def smem():
    return pl.BlockSpec(memory_space=pltpu.SMEM)


def low_lanes(rows):
    return lax.broadcasted_iota(jnp.int32, (rows, 128), 1) < HD


def flat(rows, at):
    return pltpu.roll(jnp.concatenate([rows, jnp.zeros((1, 128 - rows.shape[1]), jnp.int32)], axis=1), 16 * at, 1)


def make_plan(adj, perms, plan):
    lane = lax.broadcasted_iota(jnp.int32, (1, 128), 1)
    ids = jnp.where(lane < 16, lane, 0)
    for s in range(MAXADJ):
        ids = ids + flat(adj[s:s + 1, :], 1 + s)
    for m in range(MATCH):
        ids = ids + flat(perms[m], 1 + MAXADJ + m)
    across = lax.broadcasted_iota(jnp.int32, (128, 128), 1)
    down = lax.broadcasted_iota(jnp.int32, (128, 128), 0)

    def column(row):
        return jnp.sum(jnp.where(across == down, jnp.broadcast_to(row, (128, 128)), 0), axis=1, keepdims=True)

    ids_down = column(ids)
    before = ids_down * 128 + down < jnp.broadcast_to(ids * 128 + lane, (128, 128))
    rank = jnp.sum(jnp.where(before, 1, 0), axis=0, keepdims=True)
    order = jnp.sum(jnp.where(column(rank) == across, down, 0), axis=0, keepdims=True)
    last = jnp.sum(jnp.where(ids_down <= across, 1, 0), axis=0, keepdims=True) - 1
    plan[0:1, :] = ids
    plan[1:2, :] = order
    plan[2:3, :] = last
    plan[3:8, :] = jnp.zeros((5, 128), jnp.int32)


def loop(first, stop, act):
    def body(d, carry):
        act(d)
        return carry

    lax.fori_loop(first, stop, body, 0)


def layer_kernel(ways, xs, ys, adj_hbm, perms_hbm, counts_hbm, wq_hbm, wv_hbm, wk_hbm, cot_hbm, feats_hbm,
                 attn_ref, gx_ref, out_ref,
                 plan, counts, adj, perms, plan_rows, cot, feats, shard, wb, packed, landed, kv, kvt, qs, terms, runs, t1, t2, feats_t, gw,
                 near, line, r1_ref, r2_ref, all_ref, in_sem, w_send, w_recv, c_send, c_recv, f_send, f_recv, a_send, a_recv, p_send, p_recv, h_send, h_recv,
                 z_send, z_recv, n_send, n_recv, y_send, y_recv, g_send, g_recv):
    node = lax.axis_index("node")
    me = lax.axis_index("head")
    half = lax.rem(me, 2)
    head = me // 2
    partner = me + 1 - 2 * half
    cross = xs * CORES
    nodes = ys * cross
    y = node // cross
    near_me = lax.rem(node, cross)
    core = lax.rem(node, CORES)
    cols, width = wq_hbm.shape
    reach = ways // 2
    barrier = pltpu.get_barrier_semaphore()

    def around(d):
        return (node, lax.rem(me + d, ways))

    def across(d):
        return (lax.rem(node + d, nodes), me)

    def remote(src, dst, send_sem, recv_sem, device):
        return pltpu.make_async_remote_copy(
            src_ref=src, dst_ref=dst, send_sem=send_sem, recv_sem=recv_sem, device_id=device, device_id_type=MESH)

    loop(1, ways, lambda d: pl.semaphore_signal(barrier, inc=1, device_id=around(d), device_id_type=MESH))
    loop(1, nodes // CORES, lambda d: pl.semaphore_signal(
        barrier, inc=1, device_id=across(CORES * d), device_id_type=MESH))
    for x in range(xs):
        other = y * cross + lax.rem(near_me // CORES + x, xs) * CORES + 1 - core
        pl.semaphore_signal(barrier, inc=1, device_id=(other, me), device_id_type=MESH)
    inputs = [
        pltpu.make_async_copy(src, dst, in_sem.at[i])
        for i, (src, dst) in enumerate((
            (wq_hbm, shard.at[0]), (wv_hbm, shard.at[1]), (wk_hbm, shard.at[2]), (cot_hbm, cot),
            (feats_hbm, feats), (adj_hbm, adj), (perms_hbm, perms), (counts_hbm, counts)))
    ]
    for copy in inputs:
        copy.start()
    for copy in inputs[:4]:
        copy.wait()
    wb[0] = jnp.zeros(wb.shape[1:], wb.dtype)
    wb[pl.ds(1, 3), half] = shard[...]
    low = low_lanes(64)
    for p in range(HEADS // 2):
        pair = cot[:, 128 * p:128 * (p + 1)].astype(jnp.float32)
        first, second = pair[:64], pair[64:]
        packed[2 * p] = jnp.where(low, first, pltpu.roll(second, 64, 1)).astype(jnp.bfloat16)
        packed[2 * p + 1] = jnp.where(low, pltpu.roll(first, 64, 1), second).astype(jnp.bfloat16)
    landed[me] = packed[head]
    for copy in inputs[4:]:
        copy.wait()
    make_plan(adj, perms, plan_rows)
    plan_copy = pltpu.make_async_copy(plan_rows, plan, in_sem.at[8])
    plan_copy.start()
    for b in range(ways):
        feats_t[:, b * BLOCK:(b + 1) * BLOCK] = jnp.transpose(feats[b * BLOCK:(b + 1) * BLOCK, :])
    pl.semaphore_wait(barrier, (ways - 1) + (nodes // CORES - 1) + xs)

    w_copy = remote(shard, wb.at[pl.ds(1, 3), half], w_send, w_recv, (node, partner))
    w_copy.start()

    def served(d):
        return lax.rem(me + half * d + (1 - half) * (ways - d), ways)

    def passed(d):
        return lax.rem(partner + (1 - half) * d + half * (ways - d), ways)

    def cot_copy(d):
        down = lax.rem(me + d, 2)
        dest = lax.rem(me + (1 - down) * d + down * (ways - d), ways)
        return remote(packed.at[dest // 2], landed.at[me], c_send, c_recv.at[d], (node, dest))

    def pass_copy(d):
        block = served(d)
        return remote(landed.at[block], landed.at[block], f_send, f_recv.at[d], (node, partner))

    def tile(n):
        x = lax.rem(n // CORES, xs)
        core = lax.rem(n, CORES)
        rows = cols // CORES
        return (n // cross, pl.ds(pl.multiple_of(core * rows, rows), rows), pl.ds(pl.multiple_of(x * 128, 128), 128))

    def shard_copy(d):
        t, rows, lanes = tile(node)
        return remote(shard.at[t, rows, lanes], all_ref.at[me, t, rows, lanes], a_send, a_recv, around(d))

    def plane_copy(n, d):
        t, rows, lanes = tile(n)
        piece = all_ref.at[:, t, rows, lanes]
        return remote(piece, piece, p_send, p_recv, across(CORES * d))

    def core_copy(c):
        rows = pl.ds(pl.multiple_of(c * (cols // CORES), cols // CORES), cols // CORES)
        piece = all_ref.at[:, :, rows, :]
        return remote(piece, piece, h_send, h_recv, (node + 1 - 2 * core, me))

    carries = y < 3

    def all_bytes(rows, send_sem, recv_sem):
        return remote(rows, rows, send_sem, recv_sem, (node, partner))

    @pl.when(carries)
    def _():
        t, rows, lanes = tile(node)
        all_ref[me, t, rows, lanes] = shard[t, rows, lanes]
        loop(1, ways, lambda d: shard_copy(d).start())

    loop(1, reach, lambda d: cot_copy(d).start())
    pass_copy(0).start()

    plan_copy.wait()
    w_copy.wait()
    weights = wb[...].reshape(4 * HD, width)
    per = 4
    for c in range(ways // per):
        rows = feats[c * per * BLOCK:(c + 1) * per * BLOCK, :]
        out = lax.dot_general(rows, weights, NT, preferred_element_type=jnp.float32)
        for j in range(per):
            b = c * per + j
            part = out[j * BLOCK:(j + 1) * BLOCK]
            qs[b] = (part[:, :128].astype(jnp.bfloat16).astype(jnp.float32) * 0.125).astype(jnp.bfloat16)
            kv[b] = part[:, 128:].astype(jnp.bfloat16)
            kvt[b] = jnp.transpose(part[:, 128:]).astype(jnp.bfloat16)

    def block(b, serve):
        ids = [plan[0, s * ways + b] for s in range(SLOTS)]
        count = counts[b]
        keys = jnp.concatenate([kv[i] for i in ids], axis=0)
        keys_t = jnp.concatenate([kvt[i] if serve else kvt[i, HD:, :] for i in ids], axis=1)
        got = landed[b].astype(jnp.float32)
        cot_rows = jnp.concatenate(
            [jnp.where(low, got, 0.0), jnp.where(low, pltpu.roll(got, 64, 1), 0.0)], axis=0).astype(jnp.bfloat16)
        qc = jnp.concatenate([qs[b], cot_rows], axis=0)
        both = lax.dot_general(keys, qc, NT, preferred_element_type=jnp.float32)
        d_prob = both[:, BLOCK:]
        scores = []
        for s in range(SLOTS):
            part = both[s * BLOCK:(s + 1) * BLOCK, :BLOCK]
            scores.append(part + jnp.where(s <= count, 0.0, -1e30) if 1 <= s <= MAXADJ else part)
        scores = jnp.concatenate(scores, axis=0)
        expo = jnp.exp(scores - jnp.max(scores, axis=0, keepdims=True))
        recip = 1.0 / jnp.sum(expo, axis=0, keepdims=True)
        centre = jnp.sum(expo * d_prob, axis=0, keepdims=True) * recip
        prob = expo * recip
        d_score = prob * (d_prob - centre)
        mixed = jnp.concatenate([d_score.astype(jnp.bfloat16), prob.astype(jnp.bfloat16)], axis=1)
        if serve:
            rows = jnp.dot(keys_t, mixed, preferred_element_type=jnp.float32)
            values, d_query = rows[:HD, BLOCK:], rows[HD:, :BLOCK]
        else:
            d_query = jnp.dot(keys_t, mixed[:, :BLOCK], preferred_element_type=jnp.float32)
            values = jnp.zeros_like(d_query)
        both_t = jnp.concatenate([values, d_query * 0.125], axis=0)
        t1[b] = jnp.transpose(both_t).astype(jnp.bfloat16)
        terms[b] = jnp.dot(mixed, qc, preferred_element_type=jnp.float32).reshape(SLOTS, BLOCK, 128)

    def z_copy(d, src, dst, k):
        dest = served(d)
        return remote(src.at[dest], dst.at[head], z_send.at[k], z_recv.at[k], (node, dest))

    def arrive(d):
        source = served(d)
        remote(packed.at[0], landed.at[source], c_send, c_recv.at[d], (node, source)).wait_recv()
        pass_copy(d).start()

    def direct(k):
        @pl.when(k > 0)
        def _():
            arrive(2 * k)

        arrive(2 * k + 1)
        block(served(2 * k), True)
        block(served(2 * k + 1), True)

        @pl.when(k > 0)
        def _():
            z_copy(2 * k, t1, r1_ref, 0).start()

        z_copy(2 * k + 1, t1, r1_ref, 0).start()

        @pl.when(jnp.logical_and(carries, k == 1))
        def _():
            t, rows, lanes = tile(node)
            pieces = all_ref.at[pl.ds(0, ways - 1), t, rows, lanes]
            all_bytes(pieces, a_send, a_recv).wait()
            loop(1, nodes // CORES, lambda d: plane_copy(node, d).start())

    def second(k):
        for d in (2 * k, 2 * k + 1):
            other = landed.at[passed(d)]
            remote(other, other, f_send, f_recv.at[d], (node, partner)).wait_recv()
        block(passed(2 * k), False)
        block(passed(2 * k + 1), False)

    loop(0, reach // 2, direct)

    loop(0, reach // 2, second)

    def add(r, carry):
        run, before = carry
        entry = plan[1, r]
        here = plan[0, entry]
        keep = jnp.where(here == before, 1.0, 0.0)
        run = run * keep + terms[lax.rem(entry, ways), entry // ways]
        runs[r] = run
        return run, here

    lax.fori_loop(0, ways * SLOTS, add, (jnp.zeros((BLOCK, 128), jnp.float32), jnp.int32(-1)), unroll=8)

    def total_of(c):
        t2[c] = runs[plan[2, c]].astype(jnp.bfloat16)

    def total_and_send(j):
        d = reach - 1 - j
        total_of(served(d))
        z_copy(d, t2, r2_ref, 1).start()

    loop(0, reach - 1, total_and_send)
    total_of(me)
    for d in range(reach, ways):
        total_of(served(d))
    r1_ref[head] = t1[me]
    r2_ref[head] = t2[me]
    rows_all = ways * BLOCK
    grads = jnp.concatenate([t1[...].reshape(rows_all, 128), t2[...].reshape(rows_all, 128)], axis=1)
    outer = jnp.dot(feats_t[...], grads, preferred_element_type=jnp.float32)
    one, two = outer[:, :128], outer[:, 128:]
    lane = lax.broadcasted_iota(jnp.int32, one.shape, 1)
    first_half = half == 0
    q_part = jnp.where(first_half, pltpu.roll(one, 64, 1), pltpu.roll(one, 32, 1))
    v_part = jnp.where(first_half, pltpu.roll(two, 32, 1), two)
    k_part = jnp.where(first_half, two, pltpu.roll(two, 96, 1))
    gw[...] = jnp.transpose(jnp.where(lane < 32, q_part, jnp.where(lane < 64, v_part, k_part)))[:3 * cols]

    def near_node(d):
        return (y * cross + lax.rem(near_me + d, cross), me)

    def y_node(d):
        return (lax.rem(y + d, ys) * cross + near_me, me)

    def piece(index):
        rows = 3 * cols // CORES
        return (pl.ds(pl.multiple_of(lax.rem(index, CORES) * rows, rows), rows),
                pl.ds(pl.multiple_of(index // CORES * 128, 128), 128))

    def near_copy(d):
        rows, lanes = piece(lax.rem(near_me + d, cross))
        return remote(gw.at[rows, lanes], near.at[d], n_send, n_recv, near_node(d))

    def y_copy(d):
        return remote(near.at[0], line.at[d], y_send, y_recv, y_node(d))

    my_rows, my_lanes = piece(near_me)

    def back_copy(d):
        return remote(line.at[0], out_ref.at[my_rows, my_lanes], g_send, g_recv, near_node(d))

    loop(1, cross, lambda d: near_copy(d).start())

    carriers = 3 * xs

    @pl.when(carries)
    def _():
        all_bytes(runs.at[pl.ds(0, carriers - 1)], p_send, p_recv).wait_recv()

    @pl.when(jnp.logical_not(carries))
    def _():
        all_bytes(runs.at[pl.ds(0, carriers)], p_send, p_recv).wait_recv()

    core_copy(core).start()
    all_bytes(near.at[pl.ds(0, cross - 1)], n_send, n_recv).wait()
    total = gw[my_rows, my_lanes]
    for d in range(1, cross):
        total = total + near[d]
    near[0] = total
    loop(1, ys, lambda d: y_copy(d).start())

    all_bytes(t1.at[pl.ds(0, reach - 1)], z_send.at[0], z_recv.at[0]).wait()
    low_all = low_lanes(BLOCK)
    for p in range(HEADS // 2):
        first = r1_ref[2 * p].astype(jnp.float32)
        second_head = pltpu.roll(r1_ref[2 * p + 1].astype(jnp.float32), 64, 1)
        attn_ref[:, 128 * p:128 * (p + 1)] = jnp.where(low_all, first, second_head).astype(jnp.bfloat16)
    all_bytes(line.at[pl.ds(0, ys - 1)], y_send, y_recv).wait()
    for d in range(1, ys):
        total = total + line[d]
    line[0] = total
    out_ref[my_rows, my_lanes] = total
    loop(1, cross, lambda d: back_copy(d).start())

    core_copy(core).wait_send()
    core_copy(1 - core).wait_recv()
    grad = jnp.zeros(gx_ref.shape, jnp.float32)
    zeros = jnp.zeros((HD, width), jnp.bfloat16)
    for h in range(HEADS):
        wq = jnp.concatenate([zeros, all_ref[2 * h, 0], all_ref[2 * h + 1, 0]], axis=0)
        grad = grad + jnp.dot(r1_ref[h], wq, preferred_element_type=jnp.float32)

    all_bytes(t2.at[pl.ds(0, reach - 1)], z_send.at[1], z_recv.at[1]).wait()
    for h in range(HEADS):
        wvk = jnp.concatenate(
            [all_ref[2 * h, 1], all_ref[2 * h + 1, 1], all_ref[2 * h, 2], all_ref[2 * h + 1, 2]], axis=0)
        grad = grad + jnp.dot(r2_ref[h], wvk, preferred_element_type=jnp.float32)
    gx_ref[...] = grad.astype(jnp.bfloat16)

    all_bytes(near.at[pl.ds(0, cross - 1)], g_send, g_recv).wait()
    all_bytes(landed.at[pl.ds(0, reach - 1)], c_send, c_send).wait_send()
    all_bytes(landed.at[pl.ds(0, reach)], f_send, f_send).wait_send()

    @pl.when(carries)
    def _():
        all_bytes(runs.at[pl.ds(0, nodes // CORES - 1)], p_send, p_recv).wait_send()


def finish_kernel(attn_in, gx_in, gw_ref, attn_ref, gx_ref, gq_ref, gk_ref, gv_ref):
    cols = HD // 2
    attn_ref[...] = attn_in[...]
    gx_ref[...] = gx_in[...]
    gq_ref[...] = gw_ref[:cols]
    gv_ref[...] = gw_ref[cols:2 * cols]
    gk_ref[...] = gw_ref[2 * cols:]


def params(**kwargs):
    return pltpu.CompilerParams(vmem_limit_bytes=VMEM_BYTES, **kwargs)


def local(xs, ys, feats, cot, wq, wk, wv, adj, adj_count, perms):
    width = feats.shape[1]
    cols = wq.shape[1]
    group = feats.shape[0] // BLOCK
    ways = lax.axis_size("head")
    bf16, f32 = jnp.bfloat16, jnp.float32
    cross = xs * CORES
    nodes = xs * ys * CORES
    dma = pltpu.SemaphoreType.DMA
    sds = jax.ShapeDtypeStruct
    attn, grad_x, summed = pl.pallas_call(
        functools.partial(layer_kernel, ways, xs, ys),
        out_shape=(sds((BLOCK, width), bf16), sds((BLOCK, width), bf16), sds((3 * cols, width), f32)),
        in_specs=[hbm()] * 8,
        out_specs=(vmem(),) * 3,
        scratch_shapes=[
            pltpu.SMEM((8, 128), jnp.int32),
            pltpu.SMEM((group,), jnp.int32),
            pltpu.VMEM((MAXADJ, group), jnp.int32),
            pltpu.VMEM((MATCH, 1, group), jnp.int32),
            pltpu.VMEM((8, 128), jnp.int32),
            pltpu.VMEM((BLOCK, width), bf16),
            pltpu.VMEM((group * BLOCK, width), bf16),
            pltpu.VMEM((3, cols, width), bf16),
            pltpu.VMEM((4, 2, cols, width), bf16),
            pltpu.VMEM((HEADS, 64, 128), bf16),
            pltpu.VMEM((ways, 64, 128), bf16),
            pltpu.VMEM((group, BLOCK, 128), bf16),
            pltpu.VMEM((group, 128, BLOCK), bf16),
            pltpu.VMEM((group, BLOCK, 128), bf16),
            pltpu.VMEM((group, SLOTS, BLOCK, 128), f32),
            pltpu.VMEM((group * SLOTS, BLOCK, 128), f32),
            pltpu.VMEM((group, BLOCK, 128), bf16),
            pltpu.VMEM((group, BLOCK, 128), bf16),
            pltpu.VMEM((width, group * BLOCK), bf16),
            pltpu.VMEM((3 * cols, width), f32),
            pltpu.VMEM((cross, 3 * cols // CORES, 128), f32),
            pltpu.VMEM((ys, 3 * cols // CORES, 128), f32),
            pltpu.VMEM((HEADS, BLOCK, 128), bf16),
            pltpu.VMEM((HEADS, BLOCK, 128), bf16),
            pltpu.VMEM((ways, 3, cols, width), bf16),
            dma((9,)), dma, dma, dma, dma((ways // 2,)), dma, dma((ways // 2,)), dma, dma, dma, dma, dma, dma,
            dma((2,)), dma((2,)), dma, dma, dma, dma, dma, dma,
        ],
        compiler_params=params(collective_id=0, has_side_effects=True),
        cost_estimate=pl.CostEstimate(flops=16 * 2 * 1024 * 256 * 384, bytes_accessed=8 << 20, transcendentals=1 << 21),
    )(adj.T, perms, adj_count, wq.T, wv.T, wk.T, cot, feats)
    attn, grad_x, grad_wq, grad_wk, grad_wv = pl.pallas_call(
        finish_kernel,
        out_shape=(
            sds((BLOCK, width), bf16),
            sds((BLOCK, width), bf16),
            sds((cols, width), f32),
            sds((cols, width), f32),
            sds((cols, width), f32),
        ),
        in_specs=[vmem()] * 3,
        out_specs=(vmem(),) * 5,
        compiler_params=params(),
        cost_estimate=pl.CostEstimate(flops=0, bytes_accessed=1 << 20, transcendentals=0),
    )(attn, grad_x, summed)
    return (attn, grad_x, grad_wq.T, grad_wk.T, grad_wv.T)


def solution(mesh):
    nodes = mesh.shape["node"]
    xs = 4 if nodes >= 8 else nodes // CORES
    ys = nodes // (xs * CORES)
    return jax.shard_map(
        functools.partial(local, xs, ys),
        mesh=mesh,
        in_specs=(
            P("node", None),
            P(("node", "head"), None),
            P(None, "head"),
            P(None, "head"),
            P(None, "head"),
            P("node", None),
            P("node"),
            P(None, "node", None),
        ),
        out_specs=(
            P(("node", "head"), None),
            P(("node", "head"), None),
            P(None, "head"),
            P(None, "head"),
            P(None, "head"),
        ),
        check_vma=False,
    )
```
